32 devices in a mesh: lat: 4 (over y, core), lon: 8 (over z, x).
Axes of the slice: x: 2, y: 2, z: 4, core: 2. Of those that a mesh axis runs over, the one named last changes fastest.
Arguments:
- tracers: bfloat16 [4, 12, 256, 1024], P(None, None, 'lat', 'lon'), may hold values from -6 to 6
- weights: bfloat16 [256, 2, 1024, 128], P('lat', None, 'lon'), may hold values from -0.375 to 0.375
- src_row: int32 [256, 8, 2], P('lat', 'lon'), may hold values from 0 to 255, as said below
- src_sector: int32 [256, 8, 2], P('lat', 'lon'), may hold values from 0 to 7, as said below
- kv: float32 [11, 256, 1024], P(None, 'lat', 'lon'), may hold values from 0.02 to 0.24
- kh: float32 [256, 1024], P('lat', 'lon'), may hold values from 0.03 to 0.24
Outputs:
- advected_tracers: bfloat16 [4, 12, 256, 1024], P(None, None, 'lat', 'lon')
The draws below stay inside these ranges and needn't reach their ends.
Inputs may be any that keep to these rules, and one draw needn't show every extreme that they name: src_row[y, j, k] lies within 3 rows of y and in the latitude band of row y, from 64 * (y // 64) to 64 * (y // 64) + 63. src_sector[y, j, k] is within 2 sectors of j, periodically; among the 128 entries of one band and sector j, at most 32 name the same sector, and in every band and sector some sector is named exactly 32 times.
All inputs are finite; a program needn't handle non-finite values.
Results may differ from the reference program's by a relative error of at most 0.0049.
Values may be sent and summed in bfloat16 or wider, within the bound.
A program may use at most 64 MiB of HBM per device.

```python
import jax
import jax.numpy as jnp
from jax import lax

TRACERS = 4
LEVELS = 12
BLOCK = 128
K = 2
STEPS = 2
SUBSTEPS = 2
TY = 64
NY = 256
NX = 1024
CAP = 32
N_LAT = 4
N_LON = 8


def draw_src_row(key, part):
    rows = jnp.arange(NY, dtype=jnp.int32)
    band_start = rows // TY * TY
    offsets = jax.random.randint(key, (NY, N_LON, K), -3, 4, dtype=jnp.int32)
    target = rows[:, None, None] + offsets
    return jnp.clip(target, band_start[:, None, None], band_start[:, None, None] + TY - 1).astype(jnp.int32)


def draw_src_sector(key, part):
    device_count = N_LAT * N_LON
    request_count = TY * K
    slot_count = 4 * CAP
    device_keys = jax.random.split(jax.random.fold_in(key, 7), device_count)

    def one_tile(tile_key, sector):
        first_key, second_key, third_key = jax.random.split(tile_key, 3)
        ranks = jax.random.permutation(first_key, slot_count).astype(jnp.int32)
        forced_offset = jax.random.randint(second_key, (), -2, 3, dtype=jnp.int32)
        forced = (sector + forced_offset) % N_LON
        others = jnp.arange(4, dtype=jnp.int32)
        other_offset = others - 2 + (others >= forced_offset + 2).astype(jnp.int32)
        slot_ids = jnp.arange(slot_count, dtype=jnp.int32)
        slot_sector = (sector + other_offset[slot_ids // CAP]) % N_LON
        ordered = jnp.argsort(ranks, stable=True)
        chosen = slot_sector[ordered[:request_count - CAP]]
        listing = jnp.concatenate([jnp.full((CAP,), forced, dtype=jnp.int32), chosen.astype(jnp.int32)])
        shuffle = jax.random.permutation(third_key, request_count)
        return listing[shuffle].reshape(TY, K)
    tiles = jax.vmap(one_tile)(device_keys, jnp.arange(device_count, dtype=jnp.int32) % N_LON)
    return tiles.reshape(N_LAT, N_LON, TY, K).transpose(0, 2, 1, 3).reshape(NY, N_LON, K)


def levels(own_key, shape, cuts, least, high):
    gain, own = 1.0, jax.random.fold_in(own_key, 6)
    for dim, parts in cuts:
        heights = jnp.exp(jax.random.uniform(jax.random.fold_in(own, dim), (parts,), jnp.float32, least / len(cuts), high / len(cuts)))
        gain = gain * jnp.repeat(heights, shape[dim] // parts).reshape([-1 if axis == dim else 1 for axis in range(len(shape))])
    return gain


def gaussian(stream_key, shape, width, limit, cuts=(), kind=jnp.bfloat16):
    values = width * jax.random.normal(stream_key, shape, jnp.float32)
    if cuts:
        values = values * levels(stream_key, shape, cuts, -0.22, 0.18)
    return jnp.clip(values, -limit, limit).astype(kind)


def setup_inputs(seed: int = 0) -> dict:
    arg_keys = jax.random.split(jax.random.key(seed), 7)
    return {
        "tracers": gaussian(arg_keys[0], (TRACERS, LEVELS, NY, NX), 1.0, 6.0, ((2, 4), (3, 8))),
        "weights": gaussian(arg_keys[1], (NY, K, NX, BLOCK), (K * BLOCK) ** -0.5, 0.375, ((0, 4), (2, 8))),
        "src_row": draw_src_row(jax.random.fold_in(arg_keys[6], 71), 0),
        "src_sector": draw_src_sector(jax.random.fold_in(arg_keys[6], 71), 0),
        "kv": jnp.clip(0.02 + 0.22 * jax.random.uniform(arg_keys[4], (LEVELS - 1, NY, NX), jnp.float32) ** levels(arg_keys[4], (LEVELS - 1, NY, NX), ((1, 4), (2, 8)), -0.2, 0.2), 0.02, 0.24),
        "kh": jnp.clip(0.03 + 0.21 * jax.random.uniform(arg_keys[5], (NY, NX), jnp.float32) ** levels(arg_keys[5], (NY, NX), ((0, 4), (1, 8)), -0.2, 0.2), 0.03, 0.24),
    }


def vertical(advected, kv):
    flux = kv[None] * (advected[:, 1:] - advected[:, :-1])
    zero_flux = jnp.zeros_like(flux[:, :1])
    return advected + jnp.concatenate([flux, zero_flux], axis=1) - jnp.concatenate([zero_flux, flux], axis=1)


def smooth(field, kh):
    for substep in range(SUBSTEPS):
        padded = jnp.pad(field, ((0, 0), (0, 0), (1, 1), (0, 0)))
        beside_all = padded[:, :, :-2] + padded[:, :, 2:] + jnp.roll(field, 1, axis=3) + jnp.roll(field, -1, axis=3)
        field = field + kh * (beside_all - 4.0 * field)
    return field


def reference(tracers, weights, src_row, src_sector, kv, kh):
    channels = TRACERS * LEVELS
    weight_bands = weights.reshape(N_LAT, TY, K, N_LON, BLOCK, BLOCK)
    row_bands = src_row.reshape(N_LAT, TY, N_LON, K).astype(jnp.int32)
    sector_bands = src_sector.reshape(N_LAT, TY, N_LON, K).astype(jnp.int32)
    field = tracers
    for step in range(STEPS):
        flat = field.reshape(channels, NY, N_LON, BLOCK)

        def band_work(inputs):
            band_rows, band_sectors, band_weights = inputs
            source = flat[:, band_rows, band_sectors, :]
            return jnp.einsum("cyjkq,ykjpq->cyjp", source.astype(jnp.float32), band_weights.astype(jnp.float32), precision=lax.Precision.HIGHEST)

        result = lax.map(band_work, (row_bands, sector_bands, weight_bands))
        advected = result.transpose(1, 0, 2, 3, 4).reshape(TRACERS, LEVELS, NY, NX)
        mixed = vertical(advected, kv)
        field = smooth(mixed, kh).astype(jnp.bfloat16)
    return field
```

```python
import functools

import jax
import jax.numpy as jnp
from jax import lax
from jax.experimental import pallas as pl
from jax.experimental.pallas import tpu as pltpu
from jax.sharding import PartitionSpec as P

STEPS = 2
SUBSTEPS = 2
OFFSETS = (-2, -1, 1, 2)
CAP = 32
MESH = pl.DeviceIdType.MESH
CONTRACT_LAST = (((1,), (1,)), ((), ()))
CONTRACT_FIRST = (((0,), (0,)), ((), ()))


def one_hot(rows, row, lane):
    at_row = lax.broadcasted_iota(jnp.int32, (rows, 128), 0) == row
    at_lane = lax.broadcasted_iota(jnp.int32, (rows, 128), 1) == lane
    return jnp.where(at_row & at_lane, 1.0, 0.0)


def kernel(
    n_lat, n_lon,
    pick_ref, list_ref, field_ref, weights_ref, kv_ref, kh_ref, out_ref,
    weights_buf, asked, asked_smem, blocks_first, blocks_second, field_second, packed, h, x_halo, edge, edge_in,
    weights_sem, list_send, list_recv, list_local, block_send, block_recv,
    row_send, row_recv, edge_send, edge_recv,
):
    lat, lon = lax.axis_index("lat"), lax.axis_index("lon")
    tile_rows, channels, _ = field_ref.shape
    group = tile_rows // 4

    def sector(by):
        return lax.rem(lon + by + n_lon, n_lon)

    weights_copy = pltpu.make_async_copy(weights_ref, weights_buf, weights_sem)
    weights_copy.start()
    for step in range(STEPS):
        for sub in range(SUBSTEPS):
            h[step, sub, 0] = jnp.zeros_like(h[step, sub, 0])
            h[step, sub, tile_rows + 1] = jnp.zeros_like(h[step, sub, 0])

    barrier = pltpu.get_barrier_semaphore()
    for by in OFFSETS:
        pl.semaphore_signal(barrier, 1, device_id=(lat, sector(by)), device_id_type=MESH)

    @pl.when(lat > 0)
    def _():
        pl.semaphore_signal(barrier, 1, device_id=(lat - 1, lon), device_id_type=MESH)

    @pl.when(lat < n_lat - 1)
    def _():
        pl.semaphore_signal(barrier, 1, device_id=(lat + 1, lon), device_id_type=MESH)

    own_blocks = len(OFFSETS) * CAP
    blocks_of, field_of = (blocks_first, blocks_second), (field_ref, field_second)
    inner = jnp.where(lat > 0, 1, 0) + jnp.where(lat < n_lat - 1, 1, 0)
    pl.semaphore_wait(barrier, len(OFFSETS) + inner)

    list_copies = []
    for i, by in enumerate(OFFSETS):
        copy = pltpu.make_async_remote_copy(
            src_ref=list_ref.at[i], dst_ref=asked.at[i],
            send_sem=list_send.at[i], recv_sem=list_recv.at[i],
            device_id=(lat, sector(by)), device_id_type=MESH,
        )
        copy.start()
        list_copies.append(copy)

    def own(r, carry):
        blocks_first[own_blocks + r] = field_ref[r]
        return carry

    lax.fori_loop(0, tile_rows, own, 0, unroll=8)
    for copy in list_copies:
        copy.wait()
    local = pltpu.make_async_copy(asked, asked_smem, list_local)
    local.start()
    local.wait()

    lane = lax.broadcasted_iota(jnp.int32, (channels, 128), 1)

    for step in range(STEPS):
        block_copies, blocks, field = [], blocks_of[step], field_of[step]
        for i, by in enumerate(OFFSETS):
            def pack(s, carry, i=i):
                packed[step, i * CAP + s] = field[asked_smem[i, 0, s]]
                return carry

            lax.fori_loop(0, CAP, pack, 0, unroll=8)
            here = pl.ds(i * CAP, CAP)
            copy = pltpu.make_async_remote_copy(
                src_ref=packed.at[step, here], dst_ref=blocks.at[here],
                send_sem=block_send.at[step, i], recv_sem=block_recv.at[step, i],
                device_id=(lat, sector(-by)), device_id_type=MESH,
            )
            copy.start()
            block_copies.append(copy)
        if step == 0:
            weights_copy.wait()
        for copy in block_copies:
            copy.wait()

        def advect(y, carry):
            source = jnp.concatenate(
                [blocks[pick_ref[2 * y]], blocks[pick_ref[2 * y + 1]]], axis=1
            )
            remap = jnp.concatenate([weights_buf[y, 0], weights_buf[y, 1]], axis=1)
            advected = lax.dot_general(
                source, remap, CONTRACT_LAST, preferred_element_type=jnp.float32
            )
            flux = kv_ref[y] * (pltpu.roll(advected, channels - 1, 0) - advected)
            h[step, 0, 1 + y] = advected + flux - pltpu.roll(flux, 1, 0)
            return carry

        lax.fori_loop(0, tile_rows, advect, 0, unroll=4)

        for sub in range(SUBSTEPS):
            now = h.at[step, sub]
            up = pltpu.make_async_remote_copy(
                src_ref=now.at[1], dst_ref=now.at[tile_rows + 1],
                send_sem=row_send.at[step, sub, 0], recv_sem=row_recv.at[step, sub, 0],
                device_id=(lat - 1, lon), device_id_type=MESH,
            )
            down = pltpu.make_async_remote_copy(
                src_ref=now.at[tile_rows], dst_ref=now.at[0],
                send_sem=row_send.at[step, sub, 1], recv_sem=row_recv.at[step, sub, 1],
                device_id=(lat + 1, lon), device_id_type=MESH,
            )

            @pl.when(lat > 0)
            def _():
                up.start()

            @pl.when(lat < n_lat - 1)
            def _():
                down.start()

            total = None
            for g in range(4):
                rows = now[pl.ds(1 + g * group, group)].reshape(group * channels, 128)
                choose = one_hot(8, 2 * g, 0) + one_hot(8, 2 * g + 1, 127)
                part = lax.dot_general(
                    choose.astype(jnp.bfloat16), rows.astype(jnp.bfloat16), CONTRACT_LAST,
                    preferred_element_type=jnp.float32,
                )
                total = part if total is None else total + part
            edge[step, sub] = total
            edge_copies = []
            for i, by in enumerate((1, -1)):
                copy = pltpu.make_async_remote_copy(
                    src_ref=edge.at[step, sub], dst_ref=edge_in.at[step, sub, i],
                    send_sem=edge_send.at[step, sub, i], recv_sem=edge_recv.at[step, sub, i],
                    device_id=(lat, sector(by)), device_id_type=MESH,
                )
                copy.start()
                edge_copies.append(copy)
            for copy in edge_copies:
                copy.wait()
            beside = edge_in[step, sub].reshape(16, group * channels).astype(jnp.bfloat16)
            for g in range(4):
                place = one_hot(16, 2 * g + 1, 127) + one_hot(16, 8 + 2 * g, 0)
                part = lax.dot_general(
                    beside, place.astype(jnp.bfloat16), CONTRACT_FIRST,
                    preferred_element_type=jnp.float32,
                )
                x_halo[pl.ds(g * group, group)] = part.reshape(group, channels, 128)

            @pl.when(lat > 0)
            def _():
                up.wait_send()
                down.wait_recv()

            @pl.when(lat < n_lat - 1)
            def _():
                down.wait_send()
                up.wait_recv()

            def relax(y, carry):
                center = now[1 + y]
                halo = x_halo[y]
                west = pltpu.roll(jnp.where(lane == 127, halo, center), 1, 1)
                east = pltpu.roll(jnp.where(lane == 0, halo, center), 127, 1)
                beside_all = now[y] + now[2 + y] + west + east
                new = center + kh_ref[pl.ds(y, 1)] * (beside_all - 4.0 * center)
                if sub < SUBSTEPS - 1:
                    h[step, sub + 1, 1 + y] = new
                elif step < STEPS - 1:
                    field_second[y] = new.astype(jnp.bfloat16)
                    blocks_second[own_blocks + y] = new.astype(jnp.bfloat16)
                else:
                    out_ref[y] = new.astype(jnp.bfloat16)
                return carry

            lax.fori_loop(0, tile_rows, relax, 0, unroll=4)


def local(n_lat, n_lon, tracers, weights, src_row, src_sector, kv, kh):
    tracer_count, level_count, tile_rows, tile_cols = tracers.shape
    channels = tracer_count * level_count
    reach = src_row.shape[2]
    requests = tile_rows * reach
    row = src_row.reshape(requests) - lax.axis_index("lat") * tile_rows
    nearby = (src_sector.reshape(requests) - lax.axis_index("lon") + 2 + n_lon) % n_lon
    order = jnp.arange(requests, dtype=jnp.int32)
    earlier = (nearby[:, None] == nearby[None]) & (order[None] < order[:, None])
    rank = jnp.sum(earlier, axis=1, dtype=jnp.int32)
    slot = jnp.where(nearby > 2, nearby - 1, nearby) * CAP + rank
    pick = jnp.where(nearby == 2, len(OFFSETS) * CAP + row, slot).astype(jnp.int32)
    places = jnp.arange(len(OFFSETS) * CAP, dtype=jnp.int32)
    taken = places[:, None] == jnp.where(nearby == 2, -1, slot)[None]
    lists = jnp.sum(jnp.where(taken, row[None], 0), axis=1, dtype=jnp.int32)
    lists = jnp.pad(lists.reshape(len(OFFSETS), 1, CAP), ((0, 0), (0, 7), (0, 128 - CAP)))

    field = tracers.reshape(channels, tile_rows, tile_cols).transpose(1, 0, 2)
    kv_all = jnp.pad(kv, ((0, 1), (0, 0), (0, 0))).transpose(1, 0, 2)
    kv_all = jnp.tile(kv_all, (1, tracer_count, 1))
    bf16, f32, i32 = jnp.bfloat16, jnp.float32, jnp.int32
    vmem = pl.BlockSpec(memory_space=pltpu.VMEM)
    smem = pl.BlockSpec(memory_space=pltpu.SMEM)
    count = len(OFFSETS)
    edge_shape = (8, tile_rows // 4 * channels)
    dma = pltpu.SemaphoreType.DMA
    out = pl.pallas_call(
        functools.partial(kernel, n_lat, n_lon),
        out_shape=jax.ShapeDtypeStruct(field.shape, bf16),
        in_specs=[smem, vmem, vmem, pl.BlockSpec(memory_space=pl.ANY), vmem, vmem],
        out_specs=vmem,
        scratch_shapes=[
            pltpu.VMEM(weights.shape, bf16),
            pltpu.VMEM((count, 8, 128), i32),
            pltpu.SMEM((count, 8, 128), i32),
            pltpu.VMEM((count * CAP + tile_rows, channels, tile_cols), bf16),
            pltpu.VMEM((count * CAP + tile_rows, channels, tile_cols), bf16),
            pltpu.VMEM(field.shape, bf16),
            pltpu.VMEM((STEPS, count * CAP, channels, tile_cols), bf16),
            pltpu.VMEM((STEPS, SUBSTEPS, tile_rows + 2, channels, tile_cols), f32),
            pltpu.VMEM((tile_rows, channels, tile_cols), f32),
            pltpu.VMEM((STEPS, SUBSTEPS) + edge_shape, f32),
            pltpu.VMEM((STEPS, SUBSTEPS, 2) + edge_shape, f32),
            dma, dma((count,)), dma((count,)), dma,
            dma((STEPS, count)), dma((STEPS, count)),
            dma((STEPS, SUBSTEPS, 2)), dma((STEPS, SUBSTEPS, 2)),
            dma((STEPS, SUBSTEPS, 2)), dma((STEPS, SUBSTEPS, 2)),
        ],
        compiler_params=pltpu.CompilerParams(
            collective_id=0, has_side_effects=True, vmem_limit_bytes=44 * 1024 * 1024
        ),
    )(pick, lists, field, weights, kv_all, kh)
    return out.transpose(1, 0, 2).reshape(tracers.shape)


def solution(mesh):
    return jax.shard_map(
        functools.partial(local, mesh.shape["lat"], mesh.shape["lon"]),
        mesh=mesh,
        in_specs=(
            P(None, None, "lat", "lon"),
            P("lat", None, "lon", None),
            P("lat", "lon", None),
            P("lat", "lon", None),
            P(None, "lat", "lon"),
            P("lat", "lon"),
        ),
        out_specs=P(None, None, "lat", "lon"),
        check_vma=False,
    )
```

```python
import functools

import jax
import jax.numpy as jnp
from jax import lax
from jax.experimental import pallas as pl
from jax.experimental.pallas import tpu as pltpu
from jax.sharding import PartitionSpec as P

STEPS = 2
SUBSTEPS = 2
OFFSETS = (-2, -1, 1, 2)
CAP = 32
GROUPS = 2
CUTS = (0, 8, 20, 32)
MESH = pl.DeviceIdType.MESH
CONTRACT_LAST = (((1,), (1,)), ((), ()))
CONTRACT_FIRST = (((0,), (0,)), ((), ()))


def one_hot(rows, row, lane):
    at_row = lax.broadcasted_iota(jnp.int32, (rows, 128), 0) == row
    at_lane = lax.broadcasted_iota(jnp.int32, (rows, 128), 1) == lane
    return jnp.where(at_row & at_lane, 1.0, 0.0)


def kernel(
    n_lat, n_lon,
    pick_ref, list_ref, field_ref, weights_ref, kv_ref, kh_ref, out_ref,
    weights_buf, asked, asked_smem, blocks_a, blocks_b, blocks_c, blocks_d, field_second, packed, h, x_halo, edge, edge_in,
    weights_sem, list_send, list_recv, list_local, block_send, block_recv,
    row_send, row_recv, edge_send, edge_recv,
):
    lat, lon = lax.axis_index("lat"), lax.axis_index("lon")
    _, tile_rows, channels, _ = field_ref.shape
    group = tile_rows // 4

    def sector(by):
        return lax.rem(lon + by + n_lon, n_lon)

    weights_copy = pltpu.make_async_copy(weights_ref, weights_buf, weights_sem)
    weights_copy.start()
    for turn in range(STEPS * GROUPS):
        for sub in range(SUBSTEPS):
            h[turn, sub, 0] = jnp.zeros_like(h[turn, sub, 0])
            h[turn, sub, tile_rows + 1] = jnp.zeros_like(h[turn, sub, 0])

    barrier = pltpu.get_barrier_semaphore()
    for by in OFFSETS:
        pl.semaphore_signal(barrier, 1, device_id=(lat, sector(by)), device_id_type=MESH)

    @pl.when(lat > 0)
    def _():
        pl.semaphore_signal(barrier, 1, device_id=(lat - 1, lon), device_id_type=MESH)

    @pl.when(lat < n_lat - 1)
    def _():
        pl.semaphore_signal(barrier, 1, device_id=(lat + 1, lon), device_id_type=MESH)

    own_blocks = len(OFFSETS) * CAP
    blocks_of, field_of = (blocks_a, blocks_b, blocks_c, blocks_d), (field_ref, field_second)
    inner = jnp.where(lat > 0, 1, 0) + jnp.where(lat < n_lat - 1, 1, 0)
    pl.semaphore_wait(barrier, len(OFFSETS) + inner)

    list_copies = []
    for i, by in enumerate(OFFSETS):
        copy = pltpu.make_async_remote_copy(
            src_ref=list_ref.at[i], dst_ref=asked.at[i],
            send_sem=list_send.at[i], recv_sem=list_recv.at[i],
            device_id=(lat, sector(by)), device_id_type=MESH,
        )
        copy.start()
        list_copies.append(copy)

    def own(r, carry):
        for part in range(GROUPS):
            blocks_of[part][own_blocks + r] = field_ref[part, r]
        return carry

    lax.fori_loop(0, tile_rows, own, 0, unroll=8)
    for copy in list_copies:
        copy.wait()
    local = pltpu.make_async_copy(asked, asked_smem, list_local)
    local.start()
    local.wait()

    lane = lax.broadcasted_iota(jnp.int32, (channels, 128), 1)

    def send_blocks(turn, cut):
        step, part = divmod(turn, GROUPS)
        first, count = CUTS[cut], CUTS[cut + 1] - CUTS[cut]
        field, copies = field_of[step], []
        for i, by in enumerate(OFFSETS):
            def pack(s, carry, i=i):
                packed[turn, i * CAP + s] = field[part, asked_smem[i, 0, s]]
                return carry

            lax.fori_loop(first, first + count, pack, 0, unroll=4)
            here = pl.ds(i * CAP + first, count)
            copy = pltpu.make_async_remote_copy(
                src_ref=packed.at[turn, here], dst_ref=blocks_of[turn].at[here],
                send_sem=block_send.at[turn, cut, i], recv_sem=block_recv.at[turn, cut, i],
                device_id=(lat, sector(-by)), device_id_type=MESH,
            )
            copy.start()
            copies.append(copy)
        return copies

    cuts = len(CUTS) - 1
    block_copies = [[] for _ in range(STEPS * GROUPS)]
    for cut in range(cuts):
        block_copies[0] += send_blocks(0, cut)
    weights_copy.wait()

    for turn in range(STEPS * GROUPS):
        step, part = divmod(turn, GROUPS)
        blocks = blocks_of[turn]
        for copy in block_copies[turn]:
            copy.wait()
        if turn + 1 < STEPS * GROUPS:
            block_copies[turn + 1] += send_blocks(turn + 1, 0)

        def advect(y, carry):
            source = jnp.concatenate(
                [blocks[pick_ref[2 * y]], blocks[pick_ref[2 * y + 1]]], axis=1
            )
            remap = jnp.concatenate([weights_buf[y, 0], weights_buf[y, 1]], axis=1)
            advected = lax.dot_general(
                source, remap, CONTRACT_LAST, preferred_element_type=jnp.float32
            )
            flux = kv_ref[y] * (pltpu.roll(advected, channels - 1, 0) - advected)
            h[turn, 0, 1 + y] = advected + flux - pltpu.roll(flux, 1, 0)
            return carry

        lax.fori_loop(0, tile_rows, advect, 0, unroll=16)

        for sub in range(SUBSTEPS):
            now = h.at[turn, sub]
            up = pltpu.make_async_remote_copy(
                src_ref=now.at[1], dst_ref=now.at[tile_rows + 1],
                send_sem=row_send.at[turn, sub, 0], recv_sem=row_recv.at[turn, sub, 0],
                device_id=(lat - 1, lon), device_id_type=MESH,
            )
            down = pltpu.make_async_remote_copy(
                src_ref=now.at[tile_rows], dst_ref=now.at[0],
                send_sem=row_send.at[turn, sub, 1], recv_sem=row_recv.at[turn, sub, 1],
                device_id=(lat + 1, lon), device_id_type=MESH,
            )

            @pl.when(lat > 0)
            def _():
                up.start()

            @pl.when(lat < n_lat - 1)
            def _():
                down.start()

            total = None
            for g in range(4):
                rows = now[pl.ds(1 + g * group, group)].reshape(group * channels, 128)
                choose = one_hot(8, 2 * g, 0) + one_hot(8, 2 * g + 1, 127)
                piece = lax.dot_general(
                    choose.astype(jnp.bfloat16), rows.astype(jnp.bfloat16), CONTRACT_LAST,
                    preferred_element_type=jnp.float32,
                )
                total = piece if total is None else total + piece
            edge[turn, sub] = total
            edge_copies = []
            for i, by in enumerate((1, -1)):
                copy = pltpu.make_async_remote_copy(
                    src_ref=edge.at[turn, sub], dst_ref=edge_in.at[turn, sub, i],
                    send_sem=edge_send.at[turn, sub, i], recv_sem=edge_recv.at[turn, sub, i],
                    device_id=(lat, sector(by)), device_id_type=MESH,
                )
                copy.start()
                edge_copies.append(copy)
            if turn + 1 < STEPS * GROUPS:
                block_copies[turn + 1] += send_blocks(turn + 1, 1 + sub)
            for copy in edge_copies:
                copy.wait()
            beside = edge_in[turn, sub].reshape(16, group * channels).astype(jnp.bfloat16)
            for g in range(4):
                place = one_hot(16, 2 * g + 1, 127) + one_hot(16, 8 + 2 * g, 0)
                piece = lax.dot_general(
                    beside, place.astype(jnp.bfloat16), CONTRACT_FIRST,
                    preferred_element_type=jnp.float32,
                )
                x_halo[pl.ds(g * group, group)] = piece.reshape(group, channels, 128)

            @pl.when(lat > 0)
            def _():
                up.wait_send()
                down.wait_recv()

            @pl.when(lat < n_lat - 1)
            def _():
                down.wait_send()
                up.wait_recv()

            def relax(y, carry):
                center = now[1 + y]
                halo = x_halo[y]
                west = pltpu.roll(jnp.where(lane == 127, halo, center), 1, 1)
                east = pltpu.roll(jnp.where(lane == 0, halo, center), 127, 1)
                beside_all = now[y] + now[2 + y] + west + east
                new = center + kh_ref[pl.ds(y, 1)] * (beside_all - 4.0 * center)
                if sub < SUBSTEPS - 1:
                    h[turn, sub + 1, 1 + y] = new
                elif step < STEPS - 1:
                    field_second[part, y] = new.astype(jnp.bfloat16)
                    blocks_of[GROUPS + part][own_blocks + y] = new.astype(jnp.bfloat16)
                else:
                    out_ref[part, y] = new.astype(jnp.bfloat16)
                return carry

            lax.fori_loop(0, tile_rows, relax, 0, unroll=16)


def local(n_lat, n_lon, tracers, weights, src_row, src_sector, kv, kh):
    tracer_count, level_count, tile_rows, tile_cols = tracers.shape
    channels = tracer_count // GROUPS * level_count
    reach = src_row.shape[2]
    requests = tile_rows * reach
    row = src_row.reshape(requests) - lax.axis_index("lat") * tile_rows
    nearby = (src_sector.reshape(requests) - lax.axis_index("lon") + 2 + n_lon) % n_lon
    order = jnp.arange(requests, dtype=jnp.int32)
    earlier = (nearby[:, None] == nearby[None]) & (order[None] < order[:, None])
    rank = jnp.sum(earlier, axis=1, dtype=jnp.int32)
    slot = jnp.where(nearby > 2, nearby - 1, nearby) * CAP + rank
    pick = jnp.where(nearby == 2, len(OFFSETS) * CAP + row, slot).astype(jnp.int32)
    places = jnp.arange(len(OFFSETS) * CAP, dtype=jnp.int32)
    taken = places[:, None] == jnp.where(nearby == 2, -1, slot)[None]
    lists = jnp.sum(jnp.where(taken, row[None], 0), axis=1, dtype=jnp.int32)
    lists = jnp.pad(lists.reshape(len(OFFSETS), 1, CAP), ((0, 0), (0, 7), (0, 128 - CAP)))

    field = tracers.reshape(GROUPS, channels, tile_rows, tile_cols).transpose(0, 2, 1, 3)
    kv_all = jnp.pad(kv, ((0, 1), (0, 0), (0, 0))).transpose(1, 0, 2)
    kv_all = jnp.tile(kv_all, (1, tracer_count // GROUPS, 1))
    bf16, f32, i32 = jnp.bfloat16, jnp.float32, jnp.int32
    vmem = pl.BlockSpec(memory_space=pltpu.VMEM)
    smem = pl.BlockSpec(memory_space=pltpu.SMEM)
    count, turns = len(OFFSETS), STEPS * GROUPS
    edge_shape = (8, tile_rows // 4 * channels)
    dma = pltpu.SemaphoreType.DMA
    out = pl.pallas_call(
        functools.partial(kernel, n_lat, n_lon),
        out_shape=jax.ShapeDtypeStruct(field.shape, bf16),
        in_specs=[smem, vmem, vmem, pl.BlockSpec(memory_space=pl.ANY), vmem, vmem],
        out_specs=vmem,
        scratch_shapes=[
            pltpu.VMEM(weights.shape, bf16),
            pltpu.VMEM((count, 8, 128), i32),
            pltpu.SMEM((count, 8, 128), i32),
            *[pltpu.VMEM((count * CAP + tile_rows, channels, tile_cols), bf16)] * turns,
            pltpu.VMEM(field.shape, bf16),
            pltpu.VMEM((turns, count * CAP, channels, tile_cols), bf16),
            pltpu.VMEM((turns, SUBSTEPS, tile_rows + 2, channels, tile_cols), f32),
            pltpu.VMEM((tile_rows, channels, tile_cols), f32),
            pltpu.VMEM((turns, SUBSTEPS) + edge_shape, f32),
            pltpu.VMEM((turns, SUBSTEPS, 2) + edge_shape, f32),
            dma, dma((count,)), dma((count,)), dma,
            dma((turns, len(CUTS) - 1, count)), dma((turns, len(CUTS) - 1, count)),
            dma((turns, SUBSTEPS, 2)), dma((turns, SUBSTEPS, 2)),
            dma((turns, SUBSTEPS, 2)), dma((turns, SUBSTEPS, 2)),
        ],
        compiler_params=pltpu.CompilerParams(
            collective_id=0, has_side_effects=True, vmem_limit_bytes=44 * 1024 * 1024
        ),
    )(pick, lists, field, weights, kv_all, kh)
    return out.transpose(0, 2, 1, 3).reshape(tracers.shape)


def solution(mesh):
    return jax.shard_map(
        functools.partial(local, mesh.shape["lat"], mesh.shape["lon"]),
        mesh=mesh,
        in_specs=(
            P(None, None, "lat", "lon"),
            P("lat", None, "lon", None),
            P("lat", "lon", None),
            P("lat", "lon", None),
            P(None, "lat", "lon"),
            P("lat", "lon"),
        ),
        out_specs=P(None, None, "lat", "lon"),
        check_vma=False,
    )
```

```python
import functools

import jax
import jax.numpy as jnp
from jax import lax
from jax.experimental import pallas as pl
from jax.experimental.pallas import tpu as pltpu
from jax.sharding import PartitionSpec as P

STEPS = 2
SUBSTEPS = 2
OFFSETS = (-2, -1, 1, 2)
CAP = 32
GROUPS = 2
CUTS = (0, 12, 24, 32)
MESH = pl.DeviceIdType.MESH
CONTRACT_LAST = (((1,), (1,)), ((), ()))
CONTRACT_FIRST = (((0,), (0,)), ((), ()))


def one_hot(rows, row, lane):
    at_row = lax.broadcasted_iota(jnp.int32, (rows, 128), 0) == row
    at_lane = lax.broadcasted_iota(jnp.int32, (rows, 128), 1) == lane
    return jnp.where(at_row & at_lane, 1.0, 0.0)


def kernel(
    n_lat, n_lon,
    pick_ref, list_ref, field_ref, weights_ref, kv_ref, kh_ref, out_ref,
    weights_buf, asked, asked_smem, blocks_a, blocks_b, blocks_c, blocks_d, field_second, packed, h, x_halo, edge, edge_in,
    weights_sem, list_send, list_recv, list_local, block_send, block_recv,
    row_send, row_recv, edge_send, edge_recv,
):
    lat, lon = lax.axis_index("lat"), lax.axis_index("lon")
    _, tile_rows, channels, _ = field_ref.shape
    group = tile_rows // 4

    def sector(by):
        return lax.rem(lon + by + n_lon, n_lon)

    weights_copy = pltpu.make_async_copy(weights_ref, weights_buf, weights_sem)
    weights_copy.start()
    for turn in range(STEPS * GROUPS):
        for sub in range(SUBSTEPS):
            h[turn, sub, 0] = jnp.zeros_like(h[turn, sub, 0])
            h[turn, sub, tile_rows + 1] = jnp.zeros_like(h[turn, sub, 0])

    barrier = pltpu.get_barrier_semaphore()
    for by in OFFSETS:
        pl.semaphore_signal(barrier, 1, device_id=(lat, sector(by)), device_id_type=MESH)

    @pl.when(lat > 0)
    def _():
        pl.semaphore_signal(barrier, 1, device_id=(lat - 1, lon), device_id_type=MESH)

    @pl.when(lat < n_lat - 1)
    def _():
        pl.semaphore_signal(barrier, 1, device_id=(lat + 1, lon), device_id_type=MESH)

    own_blocks = len(OFFSETS) * CAP
    blocks_of, field_of = (blocks_a, blocks_b, blocks_c, blocks_d), (field_ref, field_second)
    inner = jnp.where(lat > 0, 1, 0) + jnp.where(lat < n_lat - 1, 1, 0)
    pl.semaphore_wait(barrier, len(OFFSETS) + inner)

    list_copies = []
    for i, by in enumerate(OFFSETS):
        copy = pltpu.make_async_remote_copy(
            src_ref=list_ref.at[i], dst_ref=asked.at[i],
            send_sem=list_send.at[i], recv_sem=list_recv.at[i],
            device_id=(lat, sector(by)), device_id_type=MESH,
        )
        copy.start()
        list_copies.append(copy)

    def own(r, carry):
        for part in range(GROUPS):
            blocks_of[part][own_blocks + r] = field_ref[part, r]
        return carry

    lax.fori_loop(0, tile_rows, own, 0, unroll=8)
    for copy in list_copies:
        copy.wait()
    local = pltpu.make_async_copy(asked, asked_smem, list_local)
    local.start()
    local.wait()

    lane = lax.broadcasted_iota(jnp.int32, (channels, 128), 1)

    def send_blocks(turn, cut):
        step, part = divmod(turn, GROUPS)
        first, count = CUTS[cut], CUTS[cut + 1] - CUTS[cut]
        field, copies = field_of[step], []
        for i, by in enumerate(OFFSETS):
            def pack(s, carry, i=i):
                packed[turn, i * CAP + s] = field[part, asked_smem[i, 0, s]]
                return carry

            lax.fori_loop(first, first + count, pack, 0, unroll=4)
            here = pl.ds(i * CAP + first, count)
            copy = pltpu.make_async_remote_copy(
                src_ref=packed.at[turn, here], dst_ref=blocks_of[turn].at[here],
                send_sem=block_send.at[turn, cut, i], recv_sem=block_recv.at[turn, cut, i],
                device_id=(lat, sector(-by)), device_id_type=MESH,
            )
            copy.start()
            copies.append(copy)
        return copies

    cuts = len(CUTS) - 1
    block_copies = [[] for _ in range(STEPS * GROUPS)]
    for cut in range(cuts):
        block_copies[0] += send_blocks(0, cut)
    weights_copy.wait()

    for turn in range(STEPS * GROUPS):
        step, part = divmod(turn, GROUPS)
        blocks = blocks_of[turn]
        for copy in block_copies[turn]:
            copy.wait()
        if turn + 1 < STEPS * GROUPS:
            block_copies[turn + 1] += send_blocks(turn + 1, 0)

        def advect(y, carry):
            source = jnp.concatenate(
                [blocks[pick_ref[2 * y]], blocks[pick_ref[2 * y + 1]]], axis=1
            )
            remap = jnp.concatenate([weights_buf[y, 0], weights_buf[y, 1]], axis=1)
            advected = lax.dot_general(
                source, remap, CONTRACT_LAST, preferred_element_type=jnp.float32
            )
            flux = kv_ref[y] * (pltpu.roll(advected, channels - 1, 0) - advected)
            h[turn, 0, 1 + y] = advected + flux - pltpu.roll(flux, 1, 0)
            return carry

        lax.fori_loop(0, tile_rows, advect, 0, unroll=16)

        for sub in range(SUBSTEPS):
            now = h.at[turn, sub]
            up = pltpu.make_async_remote_copy(
                src_ref=now.at[1], dst_ref=now.at[tile_rows + 1],
                send_sem=row_send.at[turn, sub, 0], recv_sem=row_recv.at[turn, sub, 0],
                device_id=(lat - 1, lon), device_id_type=MESH,
            )
            down = pltpu.make_async_remote_copy(
                src_ref=now.at[tile_rows], dst_ref=now.at[0],
                send_sem=row_send.at[turn, sub, 1], recv_sem=row_recv.at[turn, sub, 1],
                device_id=(lat + 1, lon), device_id_type=MESH,
            )

            @pl.when(lat > 0)
            def _():
                up.start()

            @pl.when(lat < n_lat - 1)
            def _():
                down.start()

            total = None
            for g in range(4):
                rows = now[pl.ds(1 + g * group, group)].reshape(group * channels, 128)
                choose = one_hot(8, 2 * g, 0) + one_hot(8, 2 * g + 1, 127)
                piece = lax.dot_general(
                    choose.astype(jnp.bfloat16), rows.astype(jnp.bfloat16), CONTRACT_LAST,
                    preferred_element_type=jnp.float32,
                )
                total = piece if total is None else total + piece
            edge[turn, sub] = total
            edge_copies = []
            for i, by in enumerate((1, -1)):
                copy = pltpu.make_async_remote_copy(
                    src_ref=edge.at[turn, sub], dst_ref=edge_in.at[turn, sub, i],
                    send_sem=edge_send.at[turn, sub, i], recv_sem=edge_recv.at[turn, sub, i],
                    device_id=(lat, sector(by)), device_id_type=MESH,
                )
                copy.start()
                edge_copies.append(copy)
            if turn + 1 < STEPS * GROUPS:
                block_copies[turn + 1] += send_blocks(turn + 1, 1 + sub)
            for copy in edge_copies:
                copy.wait()
            beside = edge_in[turn, sub].reshape(16, group * channels).astype(jnp.bfloat16)
            for g in range(4):
                place = one_hot(16, 2 * g + 1, 127) + one_hot(16, 8 + 2 * g, 0)
                piece = lax.dot_general(
                    beside, place.astype(jnp.bfloat16), CONTRACT_FIRST,
                    preferred_element_type=jnp.float32,
                )
                x_halo[pl.ds(g * group, group)] = piece.reshape(group, channels, 128)

            @pl.when(lat > 0)
            def _():
                up.wait_send()
                down.wait_recv()

            @pl.when(lat < n_lat - 1)
            def _():
                down.wait_send()
                up.wait_recv()

            def relax(y, carry):
                center = now[1 + y]
                halo = x_halo[y]
                west = pltpu.roll(jnp.where(lane == 127, halo, center), 1, 1)
                east = pltpu.roll(jnp.where(lane == 0, halo, center), 127, 1)
                beside_all = now[y] + now[2 + y] + west + east
                new = center + kh_ref[pl.ds(y, 1)] * (beside_all - 4.0 * center)
                if sub < SUBSTEPS - 1:
                    h[turn, sub + 1, 1 + y] = new
                elif step < STEPS - 1:
                    field_second[part, y] = new.astype(jnp.bfloat16)
                    blocks_of[GROUPS + part][own_blocks + y] = new.astype(jnp.bfloat16)
                else:
                    out_ref[part, y] = new.astype(jnp.bfloat16)
                return carry

            lax.fori_loop(0, tile_rows, relax, 0, unroll=16)


def local(n_lat, n_lon, tracers, weights, src_row, src_sector, kv, kh):
    tracer_count, level_count, tile_rows, tile_cols = tracers.shape
    channels = tracer_count // GROUPS * level_count
    reach = src_row.shape[2]
    requests = tile_rows * reach
    row = src_row.reshape(requests) - lax.axis_index("lat") * tile_rows
    nearby = (src_sector.reshape(requests) - lax.axis_index("lon") + 2 + n_lon) % n_lon
    order = jnp.arange(requests, dtype=jnp.int32)
    earlier = (nearby[:, None] == nearby[None]) & (order[None] < order[:, None])
    rank = jnp.sum(earlier, axis=1, dtype=jnp.int32)
    slot = jnp.where(nearby > 2, nearby - 1, nearby) * CAP + rank
    pick = jnp.where(nearby == 2, len(OFFSETS) * CAP + row, slot).astype(jnp.int32)
    places = jnp.arange(len(OFFSETS) * CAP, dtype=jnp.int32)
    taken = places[:, None] == jnp.where(nearby == 2, -1, slot)[None]
    lists = jnp.sum(jnp.where(taken, row[None], 0), axis=1, dtype=jnp.int32)
    lists = jnp.pad(lists.reshape(len(OFFSETS), 1, CAP), ((0, 0), (0, 7), (0, 128 - CAP)))

    field = tracers.reshape(GROUPS, channels, tile_rows, tile_cols).transpose(0, 2, 1, 3)
    kv_all = jnp.pad(kv, ((0, 1), (0, 0), (0, 0))).transpose(1, 0, 2)
    kv_all = jnp.tile(kv_all, (1, tracer_count // GROUPS, 1))
    bf16, f32, i32 = jnp.bfloat16, jnp.float32, jnp.int32
    vmem = pl.BlockSpec(memory_space=pltpu.VMEM)
    smem = pl.BlockSpec(memory_space=pltpu.SMEM)
    count, turns = len(OFFSETS), STEPS * GROUPS
    edge_shape = (8, tile_rows // 4 * channels)
    dma = pltpu.SemaphoreType.DMA
    out = pl.pallas_call(
        functools.partial(kernel, n_lat, n_lon),
        out_shape=jax.ShapeDtypeStruct(field.shape, bf16),
        in_specs=[smem, vmem, vmem, pl.BlockSpec(memory_space=pl.ANY), vmem, vmem],
        out_specs=vmem,
        scratch_shapes=[
            pltpu.VMEM(weights.shape, bf16),
            pltpu.VMEM((count, 8, 128), i32),
            pltpu.SMEM((count, 8, 128), i32),
            *[pltpu.VMEM((count * CAP + tile_rows, channels, tile_cols), bf16)] * turns,
            pltpu.VMEM(field.shape, bf16),
            pltpu.VMEM((turns, count * CAP, channels, tile_cols), bf16),
            pltpu.VMEM((turns, SUBSTEPS, tile_rows + 2, channels, tile_cols), f32),
            pltpu.VMEM((tile_rows, channels, tile_cols), f32),
            pltpu.VMEM((turns, SUBSTEPS) + edge_shape, f32),
            pltpu.VMEM((turns, SUBSTEPS, 2) + edge_shape, f32),
            dma, dma((count,)), dma((count,)), dma,
            dma((turns, len(CUTS) - 1, count)), dma((turns, len(CUTS) - 1, count)),
            dma((turns, SUBSTEPS, 2)), dma((turns, SUBSTEPS, 2)),
            dma((turns, SUBSTEPS, 2)), dma((turns, SUBSTEPS, 2)),
        ],
        compiler_params=pltpu.CompilerParams(
            collective_id=0, has_side_effects=True, vmem_limit_bytes=44 * 1024 * 1024
        ),
    )(pick, lists, field, weights, kv_all, kh)
    return out.transpose(0, 2, 1, 3).reshape(tracers.shape)


def solution(mesh):
    return jax.shard_map(
        functools.partial(local, mesh.shape["lat"], mesh.shape["lon"]),
        mesh=mesh,
        in_specs=(
            P(None, None, "lat", "lon"),
            P("lat", None, "lon", None),
            P("lat", "lon", None),
            P("lat", "lon", None),
            P(None, "lat", "lon"),
            P("lat", "lon"),
        ),
        out_specs=P(None, None, "lat", "lon"),
        check_vma=False,
    )
```
